512 devices in a mesh: clip: 16 (over z), frame: 32 (over x, y, core).
Axes of the slice: x: 4, y: 4, z: 16, core: 2. Of those that a mesh axis runs over, the one named last changes fastest.
Arguments:
- tokens: bfloat16 [16, 32, 196, 1024], P('clip', 'frame'), may hold values from -6 to 6
- counts: int32 [16], P('clip'), may hold values from 1 to 32, 256 in all
- norm_gain: float32 [1024], replicated, may hold values from 0.1 to 1.9
- input_weights: bfloat16 [1024, 3072], P('frame', 'clip'), may hold values from -5 to 5
- output_weights: bfloat16 [1024, 1024], P('frame', 'clip'), may hold values from -0.1875 to 0.1875
- cotangent: bfloat16 [16, 32, 196, 1024], P('clip', 'frame'), may hold values from -6 to 6
Outputs:
- result: bfloat16 [16, 32, 196, 1024], P('clip', 'frame')
- grad_tokens: bfloat16 [16, 32, 196, 1024], P('clip', 'frame')
The draws below stay inside these ranges and needn't reach their ends.
Inputs may be any that keep to these rules, and one draw needn't show every extreme that they name: The 16 counts sum to 256.
All inputs are finite; a program needn't handle non-finite values. No bound on the sum of `counts` on one device may be relied on, other than what follows from the above.
Results may differ from the reference program's by a relative error of at most 0.006.
Values may be sent and summed in bfloat16 or wider, within the bound.
A program may use at most 64 MiB of HBM per device.

```python
import math
import jax
import jax.numpy as jnp
import numpy as np
from jax import lax

D = 1024
P_SIZE = 196
DH = 64
FRAMES = 32
CLIPS = 16
TOTAL = 256


def draw_input_weights(key, part):
    normal_key = jax.random.fold_in(key, 0)
    weights = jax.random.truncated_normal(normal_key, -4.0, 4.0, (D, 3 * D), jnp.float32) * D ** (-0.5)
    return weights.astype(jnp.bfloat16)


def block_levels(own_key, dims, cuts, least, largest):
    loudness = 1.0
    for dim, parts in cuts:
        draws = jax.random.uniform(jax.random.fold_in(jax.random.fold_in(own_key, 6), dim), (parts,), jnp.float32, least / len(cuts), largest / len(cuts))
        loudness = loudness * jnp.repeat(jnp.exp(draws), dims[dim] // parts).reshape((-1,) + (1,) * (len(dims) - 1 - dim))
    return loudness


def split_up(count, total, reach, lean):
    loads = [(1 << 20) // math.isqrt(standing ** lean) + 1 for standing in range(2, count + 1)]
    surplus, holding = total - reach - (count - 1), [1] * (count - 1)
    while surplus > 0:
        movable = [i for i in range(count - 1) if holding[i] < reach]
        mass, remaining = sum([loads[i] for i in movable]), surplus
        for i in movable:
            extra = min(reach - holding[i], max(1, remaining * loads[i] // mass), surplus)
            holding[i] = holding[i] + extra
            surplus = surplus - extra
    return np.array([reach] + holding)


def uneven_parts(stream_key, number_of, total, most, lean):
    if number_of == 2:
        one = jax.random.randint(stream_key, (), max(1, total - most), min(most, total - 1) + 1)
        return jnp.stack([one, total - one])
    sizes = jnp.asarray(split_up(number_of, total, most, lean), jnp.int32)
    twos = (number_of - 1) // 2
    donor, sink = sizes[1:1 + 2 * twos:2], sizes[2:2 + 2 * twos:2]
    room = jnp.minimum(donor - 1, most - sink)
    shifted = jax.random.randint(jax.random.fold_in(stream_key, 1), (twos,), 0, 1 << 20) % (room + 1)
    sizes = sizes.at[1:1 + 2 * twos:2].set(donor - shifted).at[2:2 + 2 * twos:2].set(sink + shifted)
    return sizes[jax.random.permutation(jax.random.fold_in(stream_key, 2), number_of)]


def bell_draw(key, dims, spread, reach, shards=(), held_as=jnp.bfloat16):
    entries = jax.random.normal(key, dims, jnp.float32) * spread
    if len(shards) > 0:
        entries = block_levels(key, dims, shards, -0.22, 0.18) * entries
    return jnp.clip(entries, min=-reach, max=reach).astype(held_as)


def setup_inputs(seed: int = 0) -> dict:
    seeds = jax.random.split(jax.random.key(seed), 7)
    tokens = bell_draw(seeds[0], (CLIPS, FRAMES, P_SIZE, D), 1.0, 6.0, ((0, 16), (1, 32)))
    counts = uneven_parts(seeds[1], CLIPS, TOTAL, FRAMES, 2).astype(jnp.int32)
    norm_gain = jnp.clip(1.0 + 0.18 * jax.random.normal(seeds[2], (D,), jnp.float32), 0.1, 1.9)
    input_weights = draw_input_weights(jax.random.fold_in(seeds[6], 71), 0)
    output_weights = bell_draw(seeds[4], (D, D), D ** -0.5, 0.1875, ((0, 32), (1, 16)))
    cotangent = bell_draw(seeds[5], (CLIPS, FRAMES, P_SIZE, D), 1.0, 6.0, ((0, 16), (1, 32)))
    return {"tokens": tokens, "counts": counts, "norm_gain": norm_gain, "input_weights": input_weights, "output_weights": output_weights, "cotangent": cotangent}


EPSILON = 1e-06
NEGATIVE = -1e+30

def layer_norm(wide_precision_rows, norm_gain):
    average = lax.optimization_barrier(jnp.mean(wide_precision_rows, axis=-1, keepdims=True))
    centred = wide_precision_rows - average
    variance = lax.optimization_barrier(jnp.mean(centred * centred, axis=-1, keepdims=True))
    return centred * lax.rsqrt(variance + EPSILON) * norm_gain

def clip_pass(tokens, cotangent, length, norm_gain, input_weights, output_weights):
    frames_total, patches, embedding_width = tokens.shape
    heads = embedding_width // DH
    score_scale = DH ** (-0.5)
    position = jnp.arange(frames_total)
    occupied_frame_slots = position < length
    frame_presence_mask = occupied_frame_slots.astype(jnp.float32)[:, None, None]
    wide_precision_rows = tokens.astype(jnp.float32)
    normed = layer_norm(wide_precision_rows, norm_gain).astype(jnp.bfloat16).reshape(-1, embedding_width)
    projected = jnp.dot(normed, input_weights, preferred_element_type=jnp.float32).astype(jnp.bfloat16)
    projected = projected.reshape(frames_total, patches, 3, heads, DH)
    query = projected[:, :, 0].astype(jnp.float32)
    keys_all = projected[:, :, 1].astype(jnp.float32)
    values = projected[:, :, 2].astype(jnp.float32)
    scores = jnp.einsum('tphd,uphd->phtu', query, keys_all) * score_scale
    scores = jnp.where(occupied_frame_slots[None, None, None, :], scores, NEGATIVE)
    highest = lax.optimization_barrier(jnp.max(scores, axis=-1, keepdims=True))
    expanded = jnp.exp(scores - highest)
    probabilities = expanded / lax.optimization_barrier(jnp.sum(expanded, axis=-1, keepdims=True))
    probs_low = lax.optimization_barrier(probabilities.astype(jnp.bfloat16)).astype(jnp.float32)
    attended = jnp.einsum('phtu,uphd->tphd', probs_low, values).astype(jnp.bfloat16)
    temporal_mixed_rows = jnp.dot(attended.reshape(-1, embedding_width), output_weights, preferred_element_type=jnp.float32)
    temporal_mixed_rows = temporal_mixed_rows.reshape(wide_precision_rows.shape)
    result = (wide_precision_rows + frame_presence_mask * temporal_mixed_rows).astype(jnp.bfloat16)
    output_gradient = (cotangent.astype(jnp.float32) * frame_presence_mask).astype(jnp.bfloat16).reshape(-1, embedding_width)
    grad_attended = jnp.dot(output_gradient, output_weights.T, preferred_element_type=jnp.float32).astype(jnp.bfloat16)
    grad_attended = grad_attended.reshape(frames_total, patches, heads, DH).astype(jnp.float32)
    attended_float = attended.astype(jnp.float32)
    grad_probs = jnp.einsum('tphd,uphd->phtu', grad_attended, values)
    row_delta = jnp.einsum('tphd,tphd->pht', grad_attended, attended_float)
    grad_scores = (probabilities * (grad_probs - row_delta[..., None])).astype(jnp.bfloat16)
    grad_scores = lax.optimization_barrier(grad_scores).astype(jnp.float32)
    grad_query = (jnp.einsum('phtu,uphd->tphd', grad_scores, keys_all) * score_scale).astype(jnp.bfloat16)
    grad_keys = (jnp.einsum('phtu,tphd->uphd', grad_scores, query) * score_scale).astype(jnp.bfloat16)
    grad_values = jnp.einsum('phtu,tphd->uphd', probs_low, grad_attended).astype(jnp.bfloat16)
    stacked = jnp.stack([grad_query, grad_keys, grad_values], axis=2).reshape(-1, 3 * embedding_width)
    grad_normed = jnp.dot(stacked, input_weights.T, preferred_element_type=jnp.float32).reshape(wide_precision_rows.shape)
    pullback = jax.vjp(lambda source: layer_norm(source, norm_gain), wide_precision_rows)[1]
    grad_rows = pullback(grad_normed)[0]
    grad_tokens = (cotangent.astype(jnp.float32) + grad_rows).astype(jnp.bfloat16)
    return (result, grad_tokens)

def reference(tokens, counts, norm_gain, input_weights, output_weights, cotangent):

    def one_clip(operands):
        return clip_pass(operands[0], operands[2], operands[1], norm_gain, input_weights, output_weights)
    result, grad_tokens = lax.map(one_clip, (tokens, counts, cotangent))
    return (result, grad_tokens)
```

```python
import functools
import jax, jax.numpy as jnp
from jax import lax
from jax.experimental import pallas as pl
from jax.experimental.pallas import tpu as pltpu
from jax.sharding import PartitionSpec as P

F32, BF16 = jnp.float32, jnp.bfloat16
D = 1024
ROWS = 256


def nn(a, b):
    return lax.dot_general(a, b, (((1,), (0,)), ((), ())), preferred_element_type=F32)


def nt(a, b):
    return lax.dot_general(a, b, (((1,), (1,)), ((), ())), preferred_element_type=F32)


def norm_stage(t_ref, nrm, xhat, rstd, gain_ref):
    def body(i, _):
        s = pl.ds(pl.multiple_of(i * 32, 32), 32)
        x = t_ref[pl.ds(i * 4, 4), 0].astype(F32).reshape(32, D)
        c = x - jnp.mean(x, axis=-1, keepdims=True)
        r = lax.rsqrt(jnp.mean(c * c, axis=-1, keepdims=True) + 1e-6)
        h = c * r
        xhat[s, :] = h
        rstd[s, :] = jnp.broadcast_to(r, (32, 128))
        nrm[s, :] = (h * gain_ref[...]).astype(BF16)
        return 0
    lax.fori_loop(0, 8, body, 0)


def mask_stage(cnt, t_ref, g, bias):
    def body(i, _):
        s = pl.ds(pl.multiple_of(i * 32, 32), 32)
        x = t_ref[pl.ds(i * 4, 4), 1].astype(F32).reshape(32, D)
        row = i * 32 + lax.broadcasted_iota(jnp.int32, (32, 1), 0)
        g[s, :] = (x * (row // 8 < cnt).astype(F32)).astype(BF16)
        u = i * 32 + lax.broadcasted_iota(jnp.int32, (32, ROWS), 0)
        t = lax.broadcasted_iota(jnp.int32, (32, ROWS), 1)
        ok = (u % 8 == t % 8) & (u // 8 < cnt)
        bias[s, :] = jnp.where(ok, 0.0, -1e30)
        return 0
    lax.fori_loop(0, 8, body, 0)


def attention_stage(proj, ga, att, dproj, bias):
    lane = lax.broadcasted_iota(jnp.int32, (ROWS, 128), 1) < 64
    eye = (lax.broadcasted_iota(jnp.int32, (128, 128), 0) == lax.broadcasted_iota(jnp.int32, (128, 128), 1)).astype(BF16)
    eye2 = (lax.broadcasted_iota(jnp.int32, (256, 256), 0) == lax.broadcasted_iota(jnp.int32, (256, 256), 1)).astype(BF16)
    top = lax.broadcasted_iota(jnp.int32, (128, ROWS), 0) < 64
    zero = jnp.zeros((ROWS, 128), BF16)

    def body(i, _):
        at = pl.multiple_of(i * 128, 128)
        q2, k2, v2 = (proj[:, pl.ds(pl.multiple_of(at + j * D, 128), 128)] for j in range(3))
        g2 = ga[:, pl.ds(at, 128)]
        kt, vt, gt = (nt(eye, a).astype(BF16) for a in (k2, v2, g2))
        gt32 = gt.astype(F32)
        parts = []
        for h in range(2):
            own = lane if h == 0 else ~lane
            st = nt(k2, jnp.where(own, q2, zero)) * 0.125 + bias[...]
            e = jnp.exp(st - jnp.max(st, axis=0, keepdims=True))
            p = e / jnp.sum(e, axis=0, keepdims=True)
            pb = p.astype(BF16)
            at_t = nn(vt, pb).astype(BF16)
            prod = gt32 * at_t.astype(F32)
            delta = jnp.sum(prod[h * 64:h * 64 + 64], axis=0, keepdims=True)
            ds = (p * (nt(v2, jnp.where(own, g2, zero)) - delta)).astype(BF16)
            parts.append((at_t, (nn(kt, ds) * 0.125).astype(BF16), nn(ds, q2) * 0.125, nn(pb, g2)))
        a, b = parts
        att[:, pl.ds(at, 128)] = nt(eye2, jnp.where(top, a[0], b[0])).astype(BF16)
        dproj[:, pl.ds(at, 128)] = nt(eye2, jnp.where(top, a[1], b[1])).astype(BF16)
        dproj[:, pl.ds(pl.multiple_of(at + D, 128), 128)] = jnp.where(lane, a[2], b[2]).astype(BF16)
        dproj[:, pl.ds(pl.multiple_of(at + 2 * D, 128), 128)] = jnp.where(lane, a[3], b[3]).astype(BF16)
        return 0
    lax.fori_loop(0, 8, body, 0)


def project_stage(nrm, w_ref, proj):
    def body(n, _):
        c = pl.ds(pl.multiple_of(n * 512, 512), 512)
        proj[:, c] = nn(nrm[...], w_ref[:, c]).astype(BF16)
        return 0
    lax.fori_loop(0, 6, body, 0)


def grad_attended_stage(g, w_ref, ga):
    def body(n, _):
        c = pl.ds(pl.multiple_of(n * 256, 256), 256)
        ga[:, c] = nt(g[...], w_ref[c, 3 * D:4 * D]).astype(BF16)
        return 0
    lax.fori_loop(0, 4, body, 0)


def result_stage(cnt, t_ref, att, w_ref, out):
    live = (lax.broadcasted_iota(jnp.int32, (ROWS, 1), 0) // 8 < cnt).astype(F32)
    def body(n, _):
        c = pl.ds(pl.multiple_of(n * 256, 256), 256)
        m = nn(att[...], w_ref[:, pl.ds(pl.multiple_of(3 * D + n * 256, 256), 256)])
        x = t_ref[:, 0, :, c].astype(F32).reshape(ROWS, 256)
        out[:, 0, :, c] = (x + live * m).astype(BF16).reshape(32, 8, 256)
        return 0
    lax.fori_loop(0, 4, body, 0)


def grad_stage(t_ref, dproj, w_ref, xhat, rstd, gain_ref, gn, out):
    def body(n, _):
        c = pl.ds(pl.multiple_of(n * 256, 256), 256)
        gn[:, c] = nt(dproj[...], w_ref[c, 0:3 * D])
        return 0
    lax.fori_loop(0, 4, body, 0)

    def last(i, _):
        s = pl.ds(pl.multiple_of(i * 32, 32), 32)
        h = xhat[s, :]
        dy = gn[s, :] * gain_ref[...]
        a = jnp.mean(dy, axis=-1, keepdims=True)
        b = jnp.mean(dy * h, axis=-1, keepdims=True)
        dx = rstd[s, 0:1] * (dy - a - h * b)
        f = pl.ds(i * 4, 4)
        x = t_ref[f, 1].astype(F32).reshape(32, D)
        out[f, 1] = (x + dx).astype(BF16).reshape(4, 8, D)
        return 0
    lax.fori_loop(0, 8, last, 0)


SCRATCH = [
    pltpu.VMEM((ROWS, D), BF16),
    pltpu.VMEM((ROWS, D), F32),
    pltpu.VMEM((ROWS, 128), F32),
    pltpu.VMEM((ROWS, D), BF16),
    pltpu.VMEM((ROWS, ROWS), F32),
    pltpu.VMEM((ROWS, 3 * D), BF16),
    pltpu.VMEM((ROWS, D), BF16),
    pltpu.VMEM((ROWS, D), BF16),
    pltpu.VMEM((ROWS, 3 * D), BF16),
    pltpu.VMEM((ROWS, D), F32),
]


def k2(stages, cnt_ref, gain_ref, t_ref, w_ref, out, nrm, xhat, rstd, g, bias, proj, ga, att, dproj, gn):
    cnt = cnt_ref[0]
    if 'n' in stages: norm_stage(t_ref, nrm, xhat, rstd, gain_ref)
    if 'm' in stages: mask_stage(cnt, t_ref, g, bias)
    if 'p' in stages: project_stage(nrm, w_ref, proj)
    if 'g' in stages: grad_attended_stage(g, w_ref, ga)
    if 'a' in stages: attention_stage(proj, ga, att, dproj, bias)
    if 'r' in stages: result_stage(cnt, t_ref, att, w_ref, out)
    if 'd' in stages: grad_stage(t_ref, dproj, w_ref, xhat, rstd, gain_ref, gn, out)


def call_k2(counts, gain, t, w, stages="nmpgard"):
    vm = pl.BlockSpec(memory_space=pltpu.VMEM)
    return pl.pallas_call(
        functools.partial(k2, stages),
        out_shape=jax.ShapeDtypeStruct((32, 2, 8, D), BF16),
        in_specs=[pl.BlockSpec(memory_space=pltpu.SMEM), vm, vm, vm],
        out_specs=vm,
        scratch_shapes=SCRATCH,
        compiler_params=pltpu.CompilerParams(vmem_limit_bytes=56 << 20),
        name="work_" + stages,
    )(counts, gain.reshape(1, D), t, w)


MESH = pl.DeviceIdType.MESH
WORKERS = 25


def worker_of(f):
    chip, core = f // 2, f % 2
    return (1 - core) * chip + core * (16 + (13 * chip) % 16)


def spot_of(j):
    return (2 * j) if j < 16 else 2 * ((5 * (j - 16)) % 16) + 1


def greet(peers):
    barrier = pltpu.get_barrier_semaphore()
    for peer in peers:
        pl.semaphore_signal(barrier, inc=1, device_id=peer, device_id_type=MESH)
    pl.semaphore_wait(barrier, len(peers))


def gather_kernel(tok_ref, cot_ref, win_ref, wout_ref, t_ref, w_ref, xs, wz, wl,
                  tx_send, tx_recv, own_sem, z_send, z_recv, s_send, s_recv):
    c, f = lax.axis_index("clip"), lax.axis_index("frame")
    core = f % 2
    barrier = pltpu.get_barrier_semaphore()

    def hail(i, _):
        pl.semaphore_signal(barrier, inc=1, device_id=(c, (f + i) % 32), device_id_type=MESH)
        return 0
    lax.fori_loop(1, 32, hail, 0)
    zs = [(c + d) % 16 for d in (4, 12, 8, 1, 15, 2, 14)]
    for z in zs:
        pl.semaphore_signal(barrier, inc=1, device_id=(z, f), device_id_type=MESH)
    r, q = c % 4, c // 4
    wz[r, q, :, 0:192] = win_ref[...]
    wz[r, q, :, 192:256] = wout_ref[...]
    for src, at in ((tok_ref, 0), (cot_ref, 1)):
        xs[0:24, at] = src[0:192].reshape(24, 8, D)
        xs[24, at, 0:4] = src[192:196]
        xs[24, at, 4:8] = jnp.zeros((4, D), BF16)
    pl.semaphore_wait(barrier, 38)

    def far(k):
        return pltpu.make_async_remote_copy(
            src_ref=wz.at[r, q], dst_ref=wz.at[r, q], send_sem=z_send.at[k], recv_sem=z_recv.at[k],
            device_id=(zs[k], f), device_id_type=MESH)

    for k in range(3):
        far(k).start()

    def tx(i):
        peer = (f + i) % 32
        j = worker_of(peer)
        return j, pltpu.make_async_remote_copy(
            src_ref=xs.at[jnp.minimum(j, WORKERS - 1)], dst_ref=t_ref.at[f], send_sem=tx_send.at[i], recv_sem=tx_recv.at[i],
            device_id=(c, peer), device_id_type=MESH)

    mine = worker_of(f)

    def tx_start(i, _):
        j, copy = tx(i)

        @pl.when(j < WORKERS)
        def _():
            copy.start()
        return 0
    lax.fori_loop(1, 32, tx_start, 0)
    own = pltpu.make_async_copy(xs.at[jnp.minimum(mine, WORKERS - 1)], t_ref.at[f], own_sem)
    own.start()

    for k in range(3):
        far(k).wait_recv()

    def near(k):
        return pltpu.make_async_remote_copy(
            src_ref=wz.at[r], dst_ref=wz.at[r], send_sem=z_send.at[k], recv_sem=z_recv.at[k],
            device_id=(zs[k], f), device_id_type=MESH)

    for k in range(3, 6):
        near(k).start()
    for k in range(3, 6):
        near(k).wait_recv()

    low = lax.broadcasted_iota(jnp.int32, (32, 128), 1) < 64
    for m in range(8):
        pair = []
        for z in (2 * m, 2 * m + 1):
            for h in range(2):
                pair.append(wz[z % 4, z // 4, :, 128 * h:128 * h + 128].astype(F32))
        a0, a1, b0, b1 = pair
        turned = pltpu.roll(b0, 64, 1)
        w_ref[f, :, 384 * m:384 * m + 128] = a0.astype(BF16)
        w_ref[f, :, 384 * m + 128:384 * m + 256] = jnp.where(low, a1, turned).astype(BF16)
        w_ref[f, :, 384 * m + 256:384 * m + 384] = jnp.where(low, turned, pltpu.roll(b1, 64, 1)).astype(BF16)
        w_ref[f, :, 3 * D + 128 * m:3 * D + 128 * m + 128] = jnp.where(low, pltpu.roll(a1, 64, 1), b1).astype(BF16)

    s1, s2 = 8 - 6 * core, 2 + 6 * core
    x, y = f // 8, (f // 2) % 4
    a = x * (1 - core) + y * core
    b = y * (1 - core) + x * core

    def spot(da, db):
        return ((a + da) % 4) * s1 + ((b + db) % 4) * s2 + core

    sent = []

    def send(block, to, sem, half=None):
        ref = w_ref.at[block] if half is None else w_ref.at[block, pl.ds(16 * half, 16)]
        copy = pltpu.make_async_remote_copy(
            src_ref=ref, dst_ref=ref, send_sem=s_send.at[len(sent)], recv_sem=s_recv.at[sem],
            device_id=(c, to), device_id_type=MESH)
        copy.start()
        sent.append(copy)

    def take(block, sem, half=None):
        ref = w_ref.at[block] if half is None else w_ref.at[block, pl.ds(16 * half, 16)]
        pltpu.make_async_remote_copy(
            src_ref=ref, dst_ref=ref, send_sem=s_send.at[0], recv_sem=s_recv.at[sem],
            device_id=(c, f), device_id_type=MESH).wait_recv()

    twin = f + 1 - 2 * core
    an, ap, bn, bp = spot(-1, 0), spot(1, 0), spot(0, -1), spot(0, 1)
    row = (0, -1, 1, 2)

    def along_b(n):
        send(spot(row[n], 0), bp, 4 + 4 * n)
        send(spot(row[n], 0), bn, 4 + 4 * n + 1)

    send(f, ap, 0)
    send(f, an, 1)
    along_b(0)
    send(f, twin, 20)
    take(an, 0)
    send(an, ap, 2, 0)
    along_b(1)
    send(an, twin, 21)
    take(ap, 1)
    send(ap, an, 3, 1)
    along_b(2)
    send(ap, twin, 22)
    take(spot(2, 0), 2, 0)
    take(spot(2, 0), 3, 1)
    along_b(3)
    send(spot(2, 0), twin, 23)
    for n in range(4):
        take(spot(row[n], -1), 4 + 4 * n)
        send(spot(row[n], -1), bp, 4 + 4 * n + 2, 0)
        send(spot(row[n], -1), twin, 24 + 3 * n)
        take(spot(row[n], 1), 4 + 4 * n + 1)
        send(spot(row[n], 1), bn, 4 + 4 * n + 3, 1)
        send(spot(row[n], 1), twin, 25 + 3 * n)
    for n in range(4):
        take(spot(row[n], 2), 4 + 4 * n + 2, 0)
        take(spot(row[n], 2), 4 + 4 * n + 3, 1)
        send(spot(row[n], 2), twin, 26 + 3 * n)
    def theirs(da, db):
        return ((b + da) % 4) * s2 + ((a + db) % 4) * s1 + 1 - core
    for n in range(4):
        take(theirs(row[n], 0), 20 + n)
    for n in range(4):
        for k, db in enumerate((-1, 1, 2)):
            take(theirs(row[n], db), 24 + 3 * n + k)

    @pl.when(mine < WORKERS)
    def _():
        def tx_wait(i, _):
            pltpu.make_async_remote_copy(
                src_ref=xs.at[0], dst_ref=t_ref.at[(f - i + 32) % 32], send_sem=tx_send.at[i], recv_sem=tx_recv.at[i],
                device_id=(c, f), device_id_type=MESH).wait_recv()
            return 0
        lax.fori_loop(1, 32, tx_wait, 0)
    own.wait()

    def tx_done(i, _):
        j, copy = tx(i)

        @pl.when(j < WORKERS)
        def _():
            copy.wait_send()
        return 0
    lax.fori_loop(1, 32, tx_done, 0)
    for k in range(3):
        far(k).wait_send()
        near(k + 3).wait_send()
    for copy in sent:
        copy.wait_send()


def return_kernel(y_ref, res_ref, grad_ref, z, send_sem, recv_sem, own_sem):
    c, f = lax.axis_index("clip"), lax.axis_index("frame")
    barrier = pltpu.get_barrier_semaphore()

    def hail(i, _):
        pl.semaphore_signal(barrier, inc=1, device_id=(c, (f + i) % 32), device_id_type=MESH)
        return 0
    lax.fori_loop(1, 32, hail, 0)
    pl.semaphore_wait(barrier, 31)
    mine = worker_of(f)
    slot = jnp.minimum(mine, WORKERS - 1)

    def copy(i):
        peer = (f + i) % 32
        return pltpu.make_async_remote_copy(
            src_ref=y_ref.at[peer], dst_ref=z.at[slot], send_sem=send_sem.at[i], recv_sem=recv_sem.at[i],
            device_id=(c, peer), device_id_type=MESH)

    own = pltpu.make_async_copy(y_ref.at[f], z.at[slot], own_sem)

    @pl.when(mine < WORKERS)
    def _():
        own.start()

        def start(i, _):
            copy(i).start()
            return 0
        lax.fori_loop(1, 32, start, 0)

    def wait(i, _):
        j = worker_of((f - i + 32) % 32)

        @pl.when(j < WORKERS)
        def _():
            pltpu.make_async_remote_copy(
                src_ref=y_ref.at[0], dst_ref=z.at[jnp.minimum(j, WORKERS - 1)], send_sem=send_sem.at[i], recv_sem=recv_sem.at[i],
                device_id=(c, f), device_id_type=MESH).wait_recv()
        return 0
    lax.fori_loop(1, 32, wait, 0)

    @pl.when(mine < WORKERS)
    def _():
        own.wait()

        def done(i, _):
            copy(i).wait_send()
            return 0
        lax.fori_loop(1, 32, done, 0)
    for ref, at in ((res_ref, 0), (grad_ref, 1)):
        ref[0:192] = z[0:24, at].reshape(192, D)
        ref[192:196] = z[24, at, 0:4]


VM = pl.BlockSpec(memory_space=pltpu.VMEM)


def per_device(tokens, counts, norm_gain, input_weights, output_weights, cotangent):
    dma = pltpu.SemaphoreType.DMA
    t, w = pl.pallas_call(
        gather_kernel,
        out_shape=(jax.ShapeDtypeStruct((32, 2, 8, D), BF16), jax.ShapeDtypeStruct((32, 32, 4 * D), BF16)),
        in_specs=[VM] * 4, out_specs=(VM, VM),
        scratch_shapes=[
            pltpu.VMEM((WORKERS, 2, 8, D), BF16), pltpu.VMEM((4, 4, 32, 256), BF16), pltpu.VMEM((8, 128), F32),
            dma((32,)), dma((32,)), dma, dma((6,)), dma((6,)), dma((36,)), dma((36,))],
        compiler_params=pltpu.CompilerParams(collective_id=0, has_side_effects=True, vmem_limit_bytes=40 << 20),
        name="gather",
    )(tokens[0, 0], cotangent[0, 0], input_weights, output_weights)
    y = call_k2(counts, norm_gain, t, w.reshape(D, 4 * D))
    res, grad = pl.pallas_call(
        return_kernel,
        out_shape=(jax.ShapeDtypeStruct((196, D), BF16),) * 2,
        in_specs=[VM], out_specs=(VM, VM),
        scratch_shapes=[pltpu.VMEM((WORKERS, 2, 8, D), BF16), dma((32,)), dma((32,)), dma],
        compiler_params=pltpu.CompilerParams(collective_id=1, has_side_effects=True, vmem_limit_bytes=40 << 20),
        name="give_back",
    )(y)
    return res[None, None], grad[None, None]


def solution(mesh):
    rows = P("clip", "frame", None, None)
    return jax.shard_map(
        per_device, mesh=mesh,
        in_specs=(rows, P("clip"), P(), P("frame", "clip"), P("frame", "clip"), rows),
        out_specs=(rows, rows), check_vma=False)
```

```python
import functools
import jax, jax.numpy as jnp
from jax import lax
from jax.experimental import pallas as pl
from jax.experimental.pallas import tpu as pltpu
from jax.sharding import PartitionSpec as P

F32, BF16 = jnp.float32, jnp.bfloat16
D = 1024
ROWS = 256


def nn(a, b):
    return lax.dot_general(a, b, (((1,), (0,)), ((), ())), preferred_element_type=F32)


def nt(a, b):
    return lax.dot_general(a, b, (((1,), (1,)), ((), ())), preferred_element_type=F32)


def norm_stage(t_ref, nrm, xhat, rstd, gain_ref):
    def body(i, _):
        s = pl.ds(pl.multiple_of(i * 32, 32), 32)
        x = t_ref[pl.ds(i * 4, 4), 0].astype(F32).reshape(32, D)
        c = x - jnp.mean(x, axis=-1, keepdims=True)
        r = lax.rsqrt(jnp.mean(c * c, axis=-1, keepdims=True) + 1e-6)
        h = c * r
        xhat[s, :] = h
        rstd[s, :] = jnp.broadcast_to(r, (32, 128))
        nrm[s, :] = (h * gain_ref[...]).astype(BF16)
        return 0
    lax.fori_loop(0, 8, body, 0)


def mask_stage(cnt, t_ref, g, bias):
    def body(i, _):
        s = pl.ds(pl.multiple_of(i * 32, 32), 32)
        x = t_ref[pl.ds(i * 4, 4), 1].astype(F32).reshape(32, D)
        row = i * 32 + lax.broadcasted_iota(jnp.int32, (32, 1), 0)
        g[s, :] = (x * (row // 8 < cnt).astype(F32)).astype(BF16)
        u = i * 32 + lax.broadcasted_iota(jnp.int32, (32, ROWS), 0)
        t = lax.broadcasted_iota(jnp.int32, (32, ROWS), 1)
        ok = (u % 8 == t % 8) & (u // 8 < cnt)
        bias[s, :] = jnp.where(ok, 0.0, -1e30)
        return 0
    lax.fori_loop(0, 8, body, 0)


def attention_stage(proj, ga, att, dproj, bias):
    lane = lax.broadcasted_iota(jnp.int32, (ROWS, 128), 1) < 64
    eye = (lax.broadcasted_iota(jnp.int32, (128, 128), 0) == lax.broadcasted_iota(jnp.int32, (128, 128), 1)).astype(BF16)
    eye2 = (lax.broadcasted_iota(jnp.int32, (256, 256), 0) == lax.broadcasted_iota(jnp.int32, (256, 256), 1)).astype(BF16)
    top = lax.broadcasted_iota(jnp.int32, (128, ROWS), 0) < 64
    zero = jnp.zeros((ROWS, 128), BF16)

    def body(i, _):
        at = pl.multiple_of(i * 128, 128)
        q2, k2, v2 = (proj[:, pl.ds(pl.multiple_of(at + j * D, 128), 128)] for j in range(3))
        g2 = ga[:, pl.ds(at, 128)]
        kt, vt, gt = (nt(eye, a).astype(BF16) for a in (k2, v2, g2))
        gt32 = gt.astype(F32)
        parts = []
        for h in range(2):
            own = lane if h == 0 else ~lane
            st = nt(k2, jnp.where(own, q2, zero)) * 0.125 + bias[...]
            e = jnp.exp(st - jnp.max(st, axis=0, keepdims=True))
            p = e / jnp.sum(e, axis=0, keepdims=True)
            pb = p.astype(BF16)
            at_t = nn(vt, pb).astype(BF16)
            prod = gt32 * at_t.astype(F32)
            delta = jnp.sum(prod[h * 64:h * 64 + 64], axis=0, keepdims=True)
            ds = (p * (nt(v2, jnp.where(own, g2, zero)) - delta)).astype(BF16)
            parts.append((at_t, (nn(kt, ds) * 0.125).astype(BF16), nn(ds, q2) * 0.125, nn(pb, g2)))
        a, b = parts
        att[:, pl.ds(at, 128)] = nt(eye2, jnp.where(top, a[0], b[0])).astype(BF16)
        dproj[:, pl.ds(at, 128)] = nt(eye2, jnp.where(top, a[1], b[1])).astype(BF16)
        dproj[:, pl.ds(pl.multiple_of(at + D, 128), 128)] = jnp.where(lane, a[2], b[2]).astype(BF16)
        dproj[:, pl.ds(pl.multiple_of(at + 2 * D, 128), 128)] = jnp.where(lane, a[3], b[3]).astype(BF16)
        return 0
    lax.fori_loop(0, 8, body, 0)


def project_stage(nrm, w_ref, proj):
    def body(n, _):
        c = pl.ds(pl.multiple_of(n * 512, 512), 512)
        proj[:, c] = nn(nrm[...], w_ref[:, :, c].reshape(D, 512)).astype(BF16)
        return 0
    lax.fori_loop(0, 6, body, 0)


def grad_attended_stage(g, w_ref, ga):
    def body(n, _):
        c = pl.ds(pl.multiple_of(n * 256, 256), 256)
        ga[:, c] = nt(g[...], w_ref[pl.ds(n * 8, 8), :, 3 * D:4 * D].reshape(256, D)).astype(BF16)
        return 0
    lax.fori_loop(0, 4, body, 0)


def result_stage(cnt, t_ref, att, w_ref, out):
    live = (lax.broadcasted_iota(jnp.int32, (ROWS, 1), 0) // 8 < cnt).astype(F32)
    def body(n, _):
        c = pl.ds(pl.multiple_of(n * 256, 256), 256)
        m = nn(att[...], w_ref[:, :, pl.ds(pl.multiple_of(3 * D + n * 256, 256), 256)].reshape(D, 256))
        x = t_ref[:, 0, :, c].astype(F32).reshape(ROWS, 256)
        out[:, 0, :, c] = (x + live * m).astype(BF16).reshape(32, 8, 256)
        return 0
    lax.fori_loop(0, 4, body, 0)


def grad_stage(t_ref, dproj, w_ref, xhat, rstd, gain_ref, gn, out):
    def body(n, _):
        c = pl.ds(pl.multiple_of(n * 256, 256), 256)
        gn[:, c] = nt(dproj[...], w_ref[pl.ds(n * 8, 8), :, 0:3 * D].reshape(256, 3 * D))
        return 0
    lax.fori_loop(0, 4, body, 0)

    def last(i, _):
        s = pl.ds(pl.multiple_of(i * 32, 32), 32)
        h = xhat[s, :]
        dy = gn[s, :] * gain_ref[...]
        a = jnp.mean(dy, axis=-1, keepdims=True)
        b = jnp.mean(dy * h, axis=-1, keepdims=True)
        dx = rstd[s, 0:1] * (dy - a - h * b)
        f = pl.ds(i * 4, 4)
        x = t_ref[f, 1].astype(F32).reshape(32, D)
        out[f, 1] = (x + dx).astype(BF16).reshape(4, 8, D)
        return 0
    lax.fori_loop(0, 8, last, 0)


SCRATCH = [
    pltpu.VMEM((ROWS, D), BF16),
    pltpu.VMEM((ROWS, D), F32),
    pltpu.VMEM((ROWS, 128), F32),
    pltpu.VMEM((ROWS, D), BF16),
    pltpu.VMEM((ROWS, ROWS), F32),
    pltpu.VMEM((ROWS, 3 * D), BF16),
    pltpu.VMEM((ROWS, D), BF16),
    pltpu.VMEM((ROWS, D), BF16),
    pltpu.VMEM((ROWS, 3 * D), BF16),
    pltpu.VMEM((ROWS, D), F32),
]


MESH = pl.DeviceIdType.MESH
WORKERS = 25


def worker_of(f):
    chip, core = f // 2, f % 2
    return (1 - core) * chip + core * (16 + (13 * chip) % 16)


def spot_of(j):
    return (2 * j) if j < 16 else 2 * ((5 * (j - 16)) % 16) + 1


def block_kernel(cnt_ref, gain_ref, tok_hbm, cot_hbm, win_hbm, wout_hbm, res_ref, grad_ref,
                 tok_ref, cot_ref, win_ref, wout_ref, xs, t_ref, y_ref, z_ref, wz, w_ref, work,
                 in_sem, tx_send, tx_recv, own_sem, z_send, z_recv, s_send, s_recv, ry_send, ry_recv):
    c, f = lax.axis_index("clip"), lax.axis_index("frame")
    core = f % 2
    loads = [pltpu.make_async_copy(src, dst, in_sem.at[k]) for k, (src, dst) in enumerate(
        ((win_hbm, win_ref), (wout_hbm, wout_ref), (tok_hbm.at[0, 0], tok_ref), (cot_hbm.at[0, 0], cot_ref)))]
    for load in loads:
        load.start()
    barrier = pltpu.get_barrier_semaphore()

    def hail(i, _):
        pl.semaphore_signal(barrier, inc=1, device_id=(c, (f + i) % 32), device_id_type=MESH)
        return 0
    lax.fori_loop(1, 32, hail, 0)
    zs = [(c + d) % 16 for d in (4, 12, 8, 1, 15, 2, 14)]
    for z in zs:
        pl.semaphore_signal(barrier, inc=1, device_id=(z, f), device_id_type=MESH)
    for load in loads:
        load.wait()
    r, q = c % 4, c // 4
    wz[r, q, :, 0:192] = win_ref[...]
    wz[r, q, :, 192:256] = wout_ref[...]
    for src, at in ((tok_ref, 0), (cot_ref, 1)):
        xs[0:24, at] = src[0:192].reshape(24, 8, D)
        xs[24, at, 0:4] = src[192:196]
        xs[24, at, 4:8] = jnp.zeros((4, D), BF16)
    pl.semaphore_wait(barrier, 38)

    def far(k):
        return pltpu.make_async_remote_copy(
            src_ref=wz.at[r, q], dst_ref=wz.at[r, q], send_sem=z_send.at[k], recv_sem=z_recv.at[k],
            device_id=(zs[k], f), device_id_type=MESH)

    for k in range(3):
        far(k).start()

    def tx(i):
        peer = (f + i) % 32
        j = worker_of(peer)
        return j, pltpu.make_async_remote_copy(
            src_ref=xs.at[jnp.minimum(j, WORKERS - 1)], dst_ref=t_ref.at[f], send_sem=tx_send.at[i], recv_sem=tx_recv.at[i],
            device_id=(c, peer), device_id_type=MESH)

    mine = worker_of(f)

    def tx_start(i, _):
        j, copy = tx(i)

        @pl.when(j < WORKERS)
        def _():
            copy.start()
        return 0
    lax.fori_loop(1, 32, tx_start, 0)
    own = pltpu.make_async_copy(xs.at[jnp.minimum(mine, WORKERS - 1)], t_ref.at[f], own_sem)
    own.start()

    for k in range(3):
        far(k).wait_recv()

    def near(k):
        return pltpu.make_async_remote_copy(
            src_ref=wz.at[r], dst_ref=wz.at[r], send_sem=z_send.at[k], recv_sem=z_recv.at[k],
            device_id=(zs[k], f), device_id_type=MESH)

    for k in range(3, 6):
        near(k).start()
    for k in range(3, 6):
        near(k).wait_recv()

    low = lax.broadcasted_iota(jnp.int32, (32, 128), 1) < 64
    for m in range(8):
        pair = []
        for z in (2 * m, 2 * m + 1):
            for h in range(2):
                pair.append(wz[z % 4, z // 4, :, 128 * h:128 * h + 128].astype(F32))
        a0, a1, b0, b1 = pair
        turned = pltpu.roll(b0, 64, 1)
        w_ref[f, :, 384 * m:384 * m + 128] = a0.astype(BF16)
        w_ref[f, :, 384 * m + 128:384 * m + 256] = jnp.where(low, a1, turned).astype(BF16)
        w_ref[f, :, 384 * m + 256:384 * m + 384] = jnp.where(low, turned, pltpu.roll(b1, 64, 1)).astype(BF16)
        w_ref[f, :, 3 * D + 128 * m:3 * D + 128 * m + 128] = jnp.where(low, pltpu.roll(a1, 64, 1), b1).astype(BF16)

    s1, s2 = 8 - 6 * core, 2 + 6 * core
    x, y = f // 8, (f // 2) % 4
    a = x * (1 - core) + y * core
    b = y * (1 - core) + x * core

    def spot(da, db):
        return ((a + da) % 4) * s1 + ((b + db) % 4) * s2 + core

    sent = []

    def send(block, to, sem, half=None):
        ref = w_ref.at[block] if half is None else w_ref.at[block, pl.ds(16 * half, 16)]
        copy = pltpu.make_async_remote_copy(
            src_ref=ref, dst_ref=ref, send_sem=s_send.at[len(sent)], recv_sem=s_recv.at[sem],
            device_id=(c, to), device_id_type=MESH)
        copy.start()
        sent.append(copy)

    def take(block, sem, half=None):
        ref = w_ref.at[block] if half is None else w_ref.at[block, pl.ds(16 * half, 16)]
        pltpu.make_async_remote_copy(
            src_ref=ref, dst_ref=ref, send_sem=s_send.at[0], recv_sem=s_recv.at[sem],
            device_id=(c, f), device_id_type=MESH).wait_recv()

    twin = f + 1 - 2 * core
    an, ap, bn, bp = spot(-1, 0), spot(1, 0), spot(0, -1), spot(0, 1)
    row = (0, -1, 1, 2)

    def along_b(n):
        send(spot(row[n], 0), bp, 4 + 4 * n)
        send(spot(row[n], 0), bn, 4 + 4 * n + 1)

    send(f, ap, 0)
    send(f, an, 1)
    along_b(0)
    send(f, twin, 20)
    take(an, 0)
    send(an, ap, 2, 0)
    along_b(1)
    send(an, twin, 21)
    take(ap, 1)
    send(ap, an, 3, 1)
    along_b(2)
    send(ap, twin, 22)
    take(spot(2, 0), 2, 0)
    take(spot(2, 0), 3, 1)
    along_b(3)
    send(spot(2, 0), twin, 23)
    for n in range(4):
        take(spot(row[n], -1), 4 + 4 * n)
        send(spot(row[n], -1), bp, 4 + 4 * n + 2, 0)
        send(spot(row[n], -1), twin, 24 + 3 * n)
        take(spot(row[n], 1), 4 + 4 * n + 1)
        send(spot(row[n], 1), bn, 4 + 4 * n + 3, 1)
        send(spot(row[n], 1), twin, 25 + 3 * n)
    for n in range(4):
        take(spot(row[n], 2), 4 + 4 * n + 2, 0)
        take(spot(row[n], 2), 4 + 4 * n + 3, 1)
        send(spot(row[n], 2), twin, 26 + 3 * n)
    def theirs(da, db):
        return ((b + da) % 4) * s2 + ((a + db) % 4) * s1 + 1 - core
    for n in range(4):
        take(theirs(row[n], 0), 20 + n)
    for n in range(4):
        for k, db in enumerate((-1, 1, 2)):
            take(theirs(row[n], db), 24 + 3 * n + k)

    @pl.when(mine < WORKERS)
    def _():
        def tx_wait(i, _):
            pltpu.make_async_remote_copy(
                src_ref=xs.at[0], dst_ref=t_ref.at[(f - i + 32) % 32], send_sem=tx_send.at[i], recv_sem=tx_recv.at[i],
                device_id=(c, f), device_id_type=MESH).wait_recv()
            return 0
        lax.fori_loop(1, 32, tx_wait, 0)
    own.wait()


    slot = jnp.minimum(mine, WORKERS - 1)

    def back(i, part):
        peer = (f + i) % 32
        return pltpu.make_async_remote_copy(
            src_ref=y_ref.at[peer, part], dst_ref=z_ref.at[part, slot], send_sem=ry_send.at[part, i],
            recv_sem=ry_recv.at[part, i], device_id=(c, peer), device_id_type=MESH)

    def give(part):
        def start(i, _):
            back(i, part).start()
            return 0
        pltpu.make_async_copy(y_ref.at[f, part], z_ref.at[part, slot], ry_send.at[part, 0]).start()
        lax.fori_loop(1, 32, start, 0)

    @pl.when(mine < WORKERS)
    def _():
        cnt = cnt_ref[0]
        nrm, xhat, rstd, g, bias, proj, ga, att, dproj, gn = work
        norm_stage(t_ref, nrm, xhat, rstd, gain_ref)
        mask_stage(cnt, t_ref, g, bias)
        project_stage(nrm, w_ref, proj)
        grad_attended_stage(g, w_ref, ga)
        attention_stage(proj, ga, att, dproj, bias)
        result_stage(cnt, t_ref, att, w_ref, y_ref)
        give(0)
        grad_stage(t_ref, dproj, w_ref, xhat, rstd, gain_ref, gn, y_ref)
        give(1)

    for part, ref in ((0, res_ref), (1, grad_ref)):
        def wait(i, _):
            j = worker_of((f - i + 32) % 32)

            @pl.when(j < WORKERS)
            def _():
                pltpu.make_async_remote_copy(
                    src_ref=y_ref.at[0, part], dst_ref=z_ref.at[part, jnp.minimum(j, WORKERS - 1)],
                    send_sem=ry_send.at[part, i], recv_sem=ry_recv.at[part, i],
                    device_id=(c, f), device_id_type=MESH).wait_recv()
            return 0
        lax.fori_loop(1, 32, wait, 0)

        @pl.when(mine < WORKERS)
        def _():
            pltpu.make_async_copy(y_ref.at[f, part], z_ref.at[part, slot], ry_send.at[part, 0]).wait()
        ref[0, 0, 0:192] = z_ref[part, 0:24].reshape(192, D)
        ref[0, 0, 192:196] = z_ref[part, 24, 0:4]

    @pl.when(mine < WORKERS)
    def _():
        def back_done(i, _):
            back(i, 0).wait_send()
            back(i, 1).wait_send()
            return 0
        lax.fori_loop(1, 32, back_done, 0)

    def tx_done(i, _):
        j, copy = tx(i)

        @pl.when(j < WORKERS)
        def _():
            copy.wait_send()
        return 0
    lax.fori_loop(1, 32, tx_done, 0)
    for k in range(3):
        far(k).wait_send()
        near(k + 3).wait_send()
    for copy in sent:
        copy.wait_send()


def per_device(tokens, counts, norm_gain, input_weights, output_weights, cotangent):
    dma = pltpu.SemaphoreType.DMA
    vm = pl.BlockSpec(memory_space=pltpu.VMEM)
    hbm = pl.BlockSpec(memory_space=pl.ANY)
    return tuple(pl.pallas_call(
        block_kernel,
        out_shape=(jax.ShapeDtypeStruct((1, 1, 196, D), BF16),) * 2,
        in_specs=[pl.BlockSpec(memory_space=pltpu.SMEM), vm, hbm, hbm, hbm, hbm], out_specs=(vm, vm),
        scratch_shapes=[
            pltpu.VMEM((196, D), BF16), pltpu.VMEM((196, D), BF16), pltpu.VMEM((32, 192), BF16), pltpu.VMEM((32, 64), BF16),
            pltpu.VMEM((WORKERS, 2, 8, D), BF16), pltpu.VMEM((32, 2, 8, D), BF16), pltpu.VMEM((32, 2, 8, D), BF16),
            pltpu.VMEM((2, WORKERS, 8, D), BF16), pltpu.VMEM((4, 4, 32, 256), BF16), pltpu.VMEM((32, 32, 4 * D), BF16),
            SCRATCH,
            dma((4,)), dma((32,)), dma((32,)), dma, dma((6,)), dma((6,)), dma((36,)), dma((36,)), dma((2, 32)), dma((2, 32))],
        compiler_params=pltpu.CompilerParams(collective_id=0, has_side_effects=True, vmem_limit_bytes=56 << 20),
        name="temporal_block",
    )(counts, norm_gain.reshape(1, D), tokens, cotangent, input_weights, output_weights))


def solution(mesh):
    rows = P("clip", "frame", None, None)
    return jax.shard_map(
        per_device, mesh=mesh,
        in_specs=(rows, P("clip"), P(), P("frame", "clip"), P("frame", "clip"), rows),
        out_specs=(rows, rows), check_vma=False)
```

```python
import functools
import jax, jax.numpy as jnp
from jax import lax
from jax.experimental import pallas as pl
from jax.experimental.pallas import tpu as pltpu
from jax.sharding import PartitionSpec as P

F32, BF16 = jnp.float32, jnp.bfloat16
D = 1024
ROWS = 256


def nn(a, b):
    return lax.dot_general(a, b, (((1,), (0,)), ((), ())), preferred_element_type=F32)


def nt(a, b):
    return lax.dot_general(a, b, (((1,), (1,)), ((), ())), preferred_element_type=F32)


def norm_stage(t_ref, nrm, xhat, rstd, gain_ref):
    def body(i, _):
        s = pl.ds(pl.multiple_of(i * 32, 32), 32)
        x = t_ref[pl.ds(i * 4, 4), 0].astype(F32).reshape(32, D)
        c = x - jnp.mean(x, axis=-1, keepdims=True)
        r = lax.rsqrt(jnp.mean(c * c, axis=-1, keepdims=True) + 1e-6)
        h = c * r
        xhat[s, :] = h
        rstd[s, :] = jnp.broadcast_to(r, (32, 128))
        nrm[s, :] = (h * gain_ref[...]).astype(BF16)
        return 0
    lax.fori_loop(0, 8, body, 0)


def mask_stage(cnt, t_ref, g, bias):
    def body(i, _):
        s = pl.ds(pl.multiple_of(i * 32, 32), 32)
        x = t_ref[pl.ds(i * 4, 4), 1].astype(F32).reshape(32, D)
        row = i * 32 + lax.broadcasted_iota(jnp.int32, (32, 1), 0)
        g[s, :] = (x * (row // 8 < cnt).astype(F32)).astype(BF16)
        u = i * 32 + lax.broadcasted_iota(jnp.int32, (32, ROWS), 0)
        t = lax.broadcasted_iota(jnp.int32, (32, ROWS), 1)
        ok = (u % 8 == t % 8) & (u // 8 < cnt)
        bias[s, :] = jnp.where(ok, 0.0, -1e30)
        return 0
    lax.fori_loop(0, 8, body, 0)


def attention_stage(proj, ga, att, dproj, bias):
    lane = lax.broadcasted_iota(jnp.int32, (ROWS, 128), 1) < 64
    top = lax.broadcasted_iota(jnp.int32, (128, ROWS), 0) < 64
    zero = jnp.zeros((ROWS, 128), BF16)
    eighth = jnp.asarray(0.125, BF16)

    def body(i, _):
        at = pl.multiple_of(i * 128, 128)
        q2, k2, v2 = (proj[:, pl.ds(pl.multiple_of(at + j * D, 128), 128)] for j in range(3))
        q2 = q2 * eighth
        g2 = ga[:, pl.ds(at, 128)]
        kt, vt, gt = k2.T * eighth, v2.T, g2.T.astype(F32)
        own = (lane, ~lane)
        st = [nt(k2, jnp.where(own[h], q2, zero)) for h in range(2)]
        dp = [nt(v2, jnp.where(own[h], g2, zero)) for h in range(2)]
        p, pb, at_t, ds = [], [], [], []
        for h in range(2):
            s = st[h] + bias[...]
            e = jnp.exp(s - jnp.max(s, axis=0, keepdims=True))
            p.append(e * (1.0 / jnp.sum(e, axis=0, keepdims=True)))
            pb.append(p[h].astype(BF16))
        for h in range(2):
            at_t.append(nn(vt, pb[h]).astype(BF16))
            delta = jnp.sum((gt * at_t[h].astype(F32))[h * 64:h * 64 + 64], axis=0, keepdims=True)
            ds.append((p[h] * (dp[h] - delta)).astype(BF16))
        dq_t = [nn(kt, ds[h]).astype(BF16) for h in range(2)]
        att[:, pl.ds(at, 128)] = jnp.where(top, *at_t).T
        dproj[:, pl.ds(at, 128)] = jnp.where(top, *dq_t).T
        dproj[:, pl.ds(pl.multiple_of(at + D, 128), 128)] = jnp.where(lane, nn(ds[0], q2), nn(ds[1], q2)).astype(BF16)
        dproj[:, pl.ds(pl.multiple_of(at + 2 * D, 128), 128)] = jnp.where(lane, nn(pb[0], g2), nn(pb[1], g2)).astype(BF16)
        return 0
    lax.fori_loop(0, 8, body, 0, unroll=4)


def columns(w, quad, lanes, width):
    four = w[:, :, pl.ds(4 * quad, 4), :, lanes]
    return jnp.concatenate([four[:, :, 2 * k:2 * k + 2].reshape(D, width) for k in range(2)], axis=1)


def project_stage(quad, nrm, w, proj):
    proj[:, pl.ds(pl.multiple_of(quad * 768, 256), 768)] = nn(nrm[...], columns(w, quad, slice(0, 384), 384)).astype(BF16)


def grad_attended_stage(quad, start, g, w, gaf):
    more = nt(g[:, pl.ds(pl.multiple_of(quad * 256, 256), 256)], columns(w, quad, slice(384, 512), 128))
    gaf[...] = more if start else gaf[...] + more


def result_stage(cnt, t_ref, att, w, out):
    live = (lax.broadcasted_iota(jnp.int32, (ROWS, 1), 0) // 8 < cnt).astype(F32)

    def body(n, _):
        c = pl.ds(pl.multiple_of(n * 256, 256), 256)
        x = t_ref[:, 0, :, c].astype(F32).reshape(ROWS, 256)
        out[:, 0, :, c] = (x + live * nn(att[...], columns(w, n, slice(384, 512), 128))).astype(BF16).reshape(32, 8, 256)
        return 0
    lax.fori_loop(0, 4, body, 0)


def grad_stage(t_ref, dproj, w, xhat, rstd, gain_ref, gn, out):
    def body(n, _):
        four = w[pl.ds(n * 4, 4), :, :, :, 0:384]
        rows = jnp.concatenate([four[:, :, 2 * m:2 * m + 2].reshape(256, 384) for m in range(8)], axis=1)
        gn[:, pl.ds(pl.multiple_of(n * 256, 256), 256)] = nt(dproj[...], rows)
        return 0
    lax.fori_loop(0, 4, body, 0)

    def last(i, _):
        s = pl.ds(pl.multiple_of(i * 32, 32), 32)
        h = xhat[s, :]
        dy = gn[s, :] * gain_ref[...]
        a = jnp.mean(dy, axis=-1, keepdims=True)
        b = jnp.mean(dy * h, axis=-1, keepdims=True)
        dx = rstd[s, 0:1] * (dy - a - h * b)
        f = pl.ds(i * 4, 4)
        x = t_ref[f, 1].astype(F32).reshape(32, D)
        out[f, 1] = (x + dx).astype(BF16).reshape(4, 8, D)
        return 0
    lax.fori_loop(0, 8, last, 0)


SCRATCH = [
    pltpu.VMEM((ROWS, D), BF16),
    pltpu.VMEM((ROWS, D), F32),
    pltpu.VMEM((ROWS, 128), F32),
    pltpu.VMEM((ROWS, D), BF16),
    pltpu.VMEM((ROWS, ROWS), F32),
    pltpu.VMEM((ROWS, 3 * D), BF16),
    pltpu.VMEM((ROWS, D), BF16),
    pltpu.VMEM((ROWS, D), BF16),
    pltpu.VMEM((ROWS, 3 * D), BF16),
    pltpu.VMEM((ROWS, D), F32),
]


MESH = pl.DeviceIdType.MESH
WORKERS = 25
VMEM_MB = 56
WAVES = (0, 3, 1, 2)


def worker_of(f):
    chip, core = f // 2, f % 2
    return (1 - core) * chip + core * (16 + (13 * chip) % 16)


def spot_of(j):
    return (2 * j) if j < 16 else 2 * ((5 * (j - 16)) % 16) + 1


def block_kernel(cnt_ref, gain_ref, tok_hbm, cot_hbm, win_hbm, wout_hbm, res_ref, grad_ref,
                 tok_ref, cot_ref, win_ref, wout_ref, xs, t_ref, y_ref, z_ref, wz, pz, w, work,
                 in_sem, tx_send, tx_recv, own_sem, z_send, z_recv, s_send, s_recv,
                 ry_send, ry_recv):
    c, f = lax.axis_index("clip"), lax.axis_index("frame")
    chip, core, par = f // 2, f % 2, c % 2
    quad = c // 4
    twin = f + 1 - 2 * core
    loads = [pltpu.make_async_copy(src, dst, in_sem.at[k]) for k, (src, dst) in enumerate(
        ((win_hbm, win_ref), (wout_hbm, wout_ref), (tok_hbm.at[0, 0], tok_ref), (cot_hbm.at[0, 0], cot_ref)))]
    for load in loads:
        load.start()
    barrier = pltpu.get_barrier_semaphore()

    def hail(i, _):
        pl.semaphore_signal(barrier, inc=1, device_id=(c, (f + i) % 32), device_id_type=MESH)
        return 0
    zs = [(c + 4) % 16, (c + 12) % 16, (c + 8) % 16] + [4 * quad + (c + d) % 4 for d in (1, 2, 3)]
    for z in zs:
        pl.semaphore_signal(barrier, inc=1, device_id=(z, f), device_id_type=MESH)
    lax.fori_loop(1, 32, hail, 0)
    for load in loads:
        load.wait()
    wz[:, 0:192] = win_ref[...]
    wz[:, 192:256] = wout_ref[...]
    for src, at in ((tok_ref, 0), (cot_ref, 1)):
        xs[0:24, at] = src[0:192].reshape(24, 8, D)
        xs[24, at, 0:4] = src[192:196]
        xs[24, at, 4:8] = jnp.zeros((4, D), BF16)
    pl.semaphore_wait(barrier, 37)

    def remote(src, dst, send_sem, recv_sem, to):
        return pltpu.make_async_remote_copy(
            src_ref=src, dst_ref=dst, send_sem=send_sem, recv_sem=recv_sem, device_id=to, device_id_type=MESH)

    swap = remote(wz.at[pl.ds(16 * (1 - par), 16)], pz, z_send.at[6], z_recv.at[6], (c + 1 - 2 * par, f))
    swap.start()

    def tx(i):
        peer = (f + i) % 32
        j = worker_of(peer)
        return j, remote(xs.at[jnp.minimum(j, WORKERS - 1)], t_ref.at[f], tx_send.at[i], tx_recv.at[i], (c, peer))

    mine = worker_of(f)

    def tx_start(i, _):
        j, copy = tx(i)

        @pl.when(j < WORKERS)
        def _():
            copy.start()
        return 0

    own = pltpu.make_async_copy(xs.at[jnp.minimum(mine, WORKERS - 1)], t_ref.at[f], own_sem)

    lax.fori_loop(1, 32, tx_start, 0)
    own.start()

    swap.wait_recv()
    low = lax.broadcasted_iota(jnp.int32, (16, 128), 1) < 64
    here = wz[pl.ds(16 * par, 16), :].astype(F32)
    there = pz[...].astype(F32)
    first, second = jnp.where(par == 0, here, there), jnp.where(par == 0, there, here)
    a0, a1, b0, b1 = first[:, :128], first[:, 128:], second[:, :128], second[:, 128:]
    turned = pltpu.roll(b0, 64, 1)
    parts = (a0, jnp.where(low, a1, turned), jnp.where(low, turned, pltpu.roll(b1, 64, 1)), jnp.where(low, pltpu.roll(a1, 64, 1), b1))
    for k in range(4):
        w[chip, core, c, :, 128 * k:128 * k + 128] = parts[k].astype(BF16)

    def far(k):
        ref = w.at[chip, core, c]
        return remote(ref, ref, z_send.at[k], z_recv.at[k], (zs[k], f))

    def near(wave, k):
        ref = w.at[chip, core, 4 * ((quad + WAVES[wave]) % 4) + c % 4]
        n = 7 + 3 * wave + k
        return remote(ref, ref, z_send.at[n], z_recv.at[n], (zs[3 + k], f))

    for k in (2, 0, 1):
        far(k).start()
    for k in range(3):
        near(0, k).start()

    s1, s2 = 4 - 3 * core, 1 + 3 * core
    x, y = chip // 4, chip % 4
    a = x * (1 - core) + y * core
    b = y * (1 - core) + x * core

    def spot(da, db):
        return ((a + da) % 4) * s1 + ((b + db) % 4) * s2

    def theirs(da, db):
        return ((b + da) % 4) * s2 + ((a + db) % 4) * s1

    sent = []
    count = [0] * 4

    def block(wave, at, half, of_core):
        first = 4 * ((quad + WAVES[wave]) % 4)
        return w.at[at, of_core, pl.ds(first, 4) if half is None else pl.ds(first + 2 * half, 2)]

    def send(wave, at, to, sem, half=None):
        ref = block(wave, at, half, core)
        copy = remote(ref, ref, s_send.at[36 * wave + count[wave]], s_recv.at[36 * wave + sem], (c, to))
        copy.start()
        sent.append(copy)
        count[wave] += 1

    def take(wave, at, sem, half=None, of_core=core):
        ref = block(wave, at, half, of_core)
        remote(ref, ref, s_send.at[36 * wave], s_recv.at[36 * wave + sem], (c, twin)).wait_recv()

    an, ap, bn, bp = spot(-1, 0), spot(1, 0), spot(0, -1), spot(0, 1)
    to_an, to_ap, to_bn, to_bp = (2 * v + core for v in (an, ap, bn, bp))
    row = (0, -1, 1, 2)

    def along_b(v, n):
        send(v, spot(row[n], 0), to_bp, 4 + 4 * n)
        send(v, spot(row[n], 0), to_bn, 4 + 4 * n + 1)

    def own_out(v):
        for k in range(3):
            near(v, k).wait_recv()
        send(v, chip, to_ap, 0)
        send(v, chip, to_an, 1)
        along_b(v, 0)
        send(v, chip, twin, 20)

    def along_a(v):
        take(v, an, 0)
        send(v, an, to_ap, 2, 0)
        along_b(v, 1)
        send(v, an, twin, 21)
        take(v, ap, 1)
        send(v, ap, to_an, 3, 1)
        along_b(v, 2)
        send(v, ap, twin, 22)

    def across_a(v):
        take(v, spot(2, 0), 2, 0)
        take(v, spot(2, 0), 3, 1)
        along_b(v, 3)
        send(v, spot(2, 0), twin, 23)

    def from_b(v, n):
        take(v, spot(row[n], -1), 4 + 4 * n)
        send(v, spot(row[n], -1), to_bp, 4 + 4 * n + 2, 0)
        send(v, spot(row[n], -1), twin, 24 + 3 * n)
        take(v, spot(row[n], 1), 4 + 4 * n + 1)
        send(v, spot(row[n], 1), to_bn, 4 + 4 * n + 3, 1)
        send(v, spot(row[n], 1), twin, 25 + 3 * n)

    def across_b(v, n):
        take(v, spot(row[n], 2), 4 + 4 * n + 2, 0)
        take(v, spot(row[n], 2), 4 + 4 * n + 3, 1)
        send(v, spot(row[n], 2), twin, 26 + 3 * n)

    def pass_on(v, k):
        far(k).wait_recv()
        for i in range(3):
            near(v, i).start()

    cnt = cnt_ref[0]
    nrm, xhat, rstd, g, bias, proj, ga, att, dproj, gn = work

    def tokens_in():
        @pl.when(mine < WORKERS)
        def _():
            def tx_wait(i, _):
                remote(xs.at[0], t_ref.at[(f - i + 32) % 32], tx_send.at[i], tx_recv.at[i], (c, twin)).wait_recv()
                return 0
            lax.fori_loop(1, 32, tx_wait, 0)
        own.wait()

        @pl.when(mine < WORKERS)
        def _():
            norm_stage(t_ref, nrm, xhat, rstd, gain_ref)
            mask_stage(cnt, t_ref, g, bias)

    def finish(v):
        for n in range(4):
            take(v, theirs(row[n], 0), 20 + n, of_core=1 - core)
        for n in range(4):
            for k, db in enumerate((-1, 1, 2)):
                take(v, theirs(row[n], db), 24 + 3 * n + k, of_core=1 - core)

        @pl.when(mine < WORKERS)
        def _():
            project_stage((quad + WAVES[v]) % 4, nrm, w, proj)
            grad_attended_stage((quad + WAVES[v]) % 4, v == 0, g, w, gn)

    pass_on(1, 0)
    pass_on(2, 1)
    own_out(0)
    pass_on(3, 2)
    along_a(0)
    own_out(1)
    own_out(2)
    from_b(0, 0)
    across_a(0)
    own_out(3)
    along_a(1)
    along_a(2)
    from_b(0, 1)
    from_b(0, 2)
    along_a(3)
    from_b(1, 0)
    from_b(2, 0)
    across_a(1)
    across_a(2)
    from_b(0, 3)
    from_b(3, 0)
    across_a(3)
    across_b(0, 0)
    from_b(1, 1)
    from_b(2, 1)
    from_b(1, 2)
    from_b(2, 2)
    across_b(0, 1)
    across_b(0, 2)
    from_b(3, 1)
    from_b(3, 2)
    from_b(1, 3)
    from_b(2, 3)
    from_b(3, 3)
    across_b(0, 3)
    for v in (1, 2):
        for n in range(4):
            across_b(v, n)
    tokens_in()
    finish(0)
    for n in range(4):
        across_b(3, n)
    for v in (1, 2, 3):
        finish(v)

    slot = jnp.minimum(mine, WORKERS - 1)

    def back(i, part):
        peer = (f + i) % 32
        return remote(y_ref.at[peer, part], z_ref.at[part, slot], ry_send.at[part, i], ry_recv.at[part, i], (c, peer))

    def give(part):
        def start(i, _):
            back(i, part).start()
            return 0
        pltpu.make_async_copy(y_ref.at[f, part], z_ref.at[part, slot], ry_send.at[part, 0]).start()
        lax.fori_loop(1, 32, start, 0)

    @pl.when(mine < WORKERS)
    def _():
        ga[...] = gn[...].astype(BF16)
        attention_stage(proj, ga, att, dproj, bias)
        result_stage(cnt, t_ref, att, w, y_ref)
        give(0)
        grad_stage(t_ref, dproj, w, xhat, rstd, gain_ref, gn, y_ref)
        give(1)

    for part, ref in ((0, res_ref), (1, grad_ref)):
        def wait(i, _):
            j = worker_of((f - i + 32) % 32)

            @pl.when(j < WORKERS)
            def _():
                remote(y_ref.at[0, part], z_ref.at[part, jnp.minimum(j, WORKERS - 1)],
                       ry_send.at[part, i], ry_recv.at[part, i], (c, twin)).wait_recv()
            return 0
        lax.fori_loop(1, 32, wait, 0)

        @pl.when(mine < WORKERS)
        def _():
            pltpu.make_async_copy(y_ref.at[f, part], z_ref.at[part, slot], ry_send.at[part, 0]).wait()
        ref[0, 0, 0:192] = z_ref[part, 0:24].reshape(192, D)
        ref[0, 0, 192:196] = z_ref[part, 24, 0:4]

    @pl.when(mine < WORKERS)
    def _():
        def back_done(i, _):
            back(i, 0).wait_send()
            back(i, 1).wait_send()
            return 0
        lax.fori_loop(1, 32, back_done, 0)

    def tx_done(i, _):
        j, copy = tx(i)

        @pl.when(j < WORKERS)
        def _():
            copy.wait_send()
        return 0
    lax.fori_loop(1, 32, tx_done, 0)

    swap.wait_send()
    for k in range(3):
        far(k).wait_send()
        for v in range(4):
            near(v, k).wait_send()
    for copy in sent:
        copy.wait_send()


def per_device(tokens, counts, norm_gain, input_weights, output_weights, cotangent):
    dma = pltpu.SemaphoreType.DMA
    vm = pl.BlockSpec(memory_space=pltpu.VMEM)
    hbm = pl.BlockSpec(memory_space=pl.ANY)
    return tuple(pl.pallas_call(
        block_kernel,
        out_shape=(jax.ShapeDtypeStruct((1, 1, 196, D), BF16),) * 2,
        in_specs=[pl.BlockSpec(memory_space=pltpu.SMEM), vm, hbm, hbm, hbm, hbm], out_specs=(vm, vm),
        scratch_shapes=[
            pltpu.VMEM((196, D), BF16), pltpu.VMEM((196, D), BF16), pltpu.VMEM((32, 192), BF16), pltpu.VMEM((32, 64), BF16),
            pltpu.VMEM((WORKERS, 2, 8, D), BF16), pltpu.VMEM((32, 2, 8, D), BF16), pltpu.VMEM((32, 2, 8, D), BF16),
            pltpu.VMEM((2, WORKERS, 8, D), BF16), pltpu.VMEM((32, 256), BF16), pltpu.VMEM((16, 256), BF16),
            pltpu.VMEM((16, 2, 16, 16, 512), BF16), SCRATCH,
            dma((4,)), dma((32,)), dma((32,)), dma, dma((19,)), dma((19,)), dma((144,)), dma((144,)),
            dma((2, 32)), dma((2, 32))],
        compiler_params=pltpu.CompilerParams(collective_id=0, has_side_effects=True, vmem_limit_bytes=VMEM_MB << 20),
        name="temporal_block",
    )(counts, norm_gain.reshape(1, D), tokens, cotangent, input_weights, output_weights))


def solution(mesh):
    rows = P("clip", "frame", None, None)
    return jax.shard_map(
        per_device, mesh=mesh,
        in_specs=(rows, P("clip"), P(), P("frame", "clip"), P("frame", "clip"), rows),
        out_specs=(rows, rows), check_vma=False)
```

```python
import functools
import jax, jax.numpy as jnp
from jax import lax
from jax.experimental import pallas as pl
from jax.experimental.pallas import tpu as pltpu
from jax.sharding import PartitionSpec as P

F32, BF16 = jnp.float32, jnp.bfloat16
D = 1024
ROWS = 256


def nn(a, b):
    return lax.dot_general(a, b, (((1,), (0,)), ((), ())), preferred_element_type=F32)


def nt(a, b):
    return lax.dot_general(a, b, (((1,), (1,)), ((), ())), preferred_element_type=F32)


def norm_stage(t_ref, nrm, xhat, rstd, gain_ref):
    def body(i, _):
        s = pl.ds(pl.multiple_of(i * 32, 32), 32)
        x = t_ref[pl.ds(i * 4, 4), 0].astype(F32).reshape(32, D)
        c = x - jnp.mean(x, axis=-1, keepdims=True)
        r = lax.rsqrt(jnp.mean(c * c, axis=-1, keepdims=True) + 1e-6)
        h = c * r
        xhat[s, :] = h
        rstd[s, :] = jnp.broadcast_to(r, (32, 128))
        nrm[s, :] = (h * gain_ref[...]).astype(BF16)
        return 0
    lax.fori_loop(0, 8, body, 0)


def mask_stage(cnt, t_ref, g, bias):
    def body(i, _):
        s = pl.ds(pl.multiple_of(i * 32, 32), 32)
        x = t_ref[pl.ds(i * 4, 4), 1].astype(F32).reshape(32, D)
        row = i * 32 + lax.broadcasted_iota(jnp.int32, (32, 1), 0)
        g[s, :] = (x * (row // 8 < cnt).astype(F32)).astype(BF16)
        u = i * 32 + lax.broadcasted_iota(jnp.int32, (32, ROWS), 0)
        t = lax.broadcasted_iota(jnp.int32, (32, ROWS), 1)
        ok = (u % 8 == t % 8) & (u // 8 < cnt)
        bias[s, :] = jnp.where(ok, 0.0, -1e30)
        return 0
    lax.fori_loop(0, 8, body, 0)


def attention_stage(proj, ga, att, dproj, bias):
    lane = lax.broadcasted_iota(jnp.int32, (ROWS, 128), 1) < 64
    top = lax.broadcasted_iota(jnp.int32, (128, ROWS), 0) < 64
    zero = jnp.zeros((ROWS, 128), BF16)
    eighth = jnp.asarray(0.125, BF16)

    def body(i, _):
        at = pl.multiple_of(i * 128, 128)
        q2, k2, v2 = (proj[:, pl.ds(pl.multiple_of(at + j * D, 128), 128)] for j in range(3))
        q2 = q2 * eighth
        g2 = ga[:, pl.ds(at, 128)]
        kt, vt, gt = k2.T * eighth, v2.T, g2.T.astype(F32)
        own = (lane, ~lane)
        st = [nt(k2, jnp.where(own[h], q2, zero)) for h in range(2)]
        dp = [nt(v2, jnp.where(own[h], g2, zero)) for h in range(2)]
        p, pb, at_t, ds = [], [], [], []
        for h in range(2):
            s = st[h] + bias[...]
            e = jnp.exp(s - jnp.max(s, axis=0, keepdims=True))
            p.append(e * (1.0 / jnp.sum(e, axis=0, keepdims=True)))
            pb.append(p[h].astype(BF16))
        for h in range(2):
            at_t.append(nn(vt, pb[h]).astype(BF16))
            delta = jnp.sum((gt * at_t[h].astype(F32))[h * 64:h * 64 + 64], axis=0, keepdims=True)
            ds.append((p[h] * (dp[h] - delta)).astype(BF16))
        dq_t = [nn(kt, ds[h]).astype(BF16) for h in range(2)]
        att[:, pl.ds(at, 128)] = jnp.where(top, *at_t).T
        dproj[:, pl.ds(at, 128)] = jnp.where(top, *dq_t).T
        dproj[:, pl.ds(pl.multiple_of(at + D, 128), 128)] = jnp.where(lane, nn(ds[0], q2), nn(ds[1], q2)).astype(BF16)
        dproj[:, pl.ds(pl.multiple_of(at + 2 * D, 128), 128)] = jnp.where(lane, nn(pb[0], g2), nn(pb[1], g2)).astype(BF16)
        return 0
    lax.fori_loop(0, 8, body, 0, unroll=8)


def columns(w, quad, lanes, width):
    four = w[:, :, pl.ds(4 * quad, 4), :, lanes]
    return jnp.concatenate([four[:, :, 2 * k:2 * k + 2].reshape(D, width) for k in range(2)], axis=1)


def project_stage(quad, nrm, w, proj):
    proj[:, pl.ds(pl.multiple_of(quad * 768, 256), 768)] = nn(nrm[...], columns(w, quad, slice(0, 384), 384)).astype(BF16)


def grad_attended_stage(quad, start, g, w, gaf):
    more = nt(g[:, pl.ds(pl.multiple_of(quad * 256, 256), 256)], columns(w, quad, slice(384, 512), 128))
    gaf[...] = more if start else gaf[...] + more


def result_stage(cnt, t_ref, att, w, out):
    live = (lax.broadcasted_iota(jnp.int32, (ROWS, 1), 0) // 8 < cnt).astype(F32)

    def body(n, _):
        c = pl.ds(pl.multiple_of(n * 256, 256), 256)
        x = t_ref[:, 0, :, c].astype(F32).reshape(ROWS, 256)
        out[:, 0, :, c] = (x + live * nn(att[...], columns(w, n, slice(384, 512), 128))).astype(BF16).reshape(32, 8, 256)
        return 0
    lax.fori_loop(0, 4, body, 0)


def grad_stage(t_ref, dproj, w, xhat, rstd, gain_ref, gn, out, first, made):
    def body(n, _):
        four = w[pl.ds(n * 4, 4), :, :, :, 0:384]
        rows = jnp.concatenate([four[:, :, 2 * m:2 * m + 2].reshape(256, 384) for m in range(8)], axis=1)
        gn[:, pl.ds(pl.multiple_of(n * 256, 256), 256)] = nt(dproj[...], rows)
        return 0
    lax.fori_loop(0, 4, body, 0)

    def last(k, _):
        i = (first + k) % 8
        s = pl.ds(pl.multiple_of(i * 32, 32), 32)
        h = xhat[s, :]
        dy = gn[s, :] * gain_ref[...]
        a = jnp.mean(dy, axis=-1, keepdims=True)
        b = jnp.mean(dy * h, axis=-1, keepdims=True)
        dx = rstd[s, 0:1] * (dy - a - h * b)
        f = pl.ds(i * 4, 4)
        x = t_ref[f, 1].astype(F32).reshape(32, D)
        out[f, 1] = (x + dx).astype(BF16).reshape(4, 8, D)
        for r in range(4):
            made(i * 4 + r)
        return 0
    lax.fori_loop(0, 8, last, 0)


SCRATCH = [
    pltpu.VMEM((ROWS, D), BF16),
    pltpu.VMEM((ROWS, D), F32),
    pltpu.VMEM((ROWS, 128), F32),
    pltpu.VMEM((ROWS, D), BF16),
    pltpu.VMEM((ROWS, ROWS), F32),
    pltpu.VMEM((ROWS, 3 * D), BF16),
    pltpu.VMEM((ROWS, D), BF16),
    pltpu.VMEM((ROWS, D), BF16),
    pltpu.VMEM((ROWS, 3 * D), BF16),
    pltpu.VMEM((ROWS, D), F32),
]


MESH = pl.DeviceIdType.MESH
WORKERS = 25
VMEM_MB = 53
WAVES = (0, 3, 1, 2)


def worker_of(f):
    chip, core = f // 2, f % 2
    return (1 - core) * chip + core * (16 + (13 * chip) % 16)


def spot_of(j):
    return (2 * j) if j < 16 else 2 * ((5 * (j - 16)) % 16) + 1


def block_kernel(cnt_hbm, gain_ref, tok_hbm, cot_hbm, win_hbm, wout_hbm, res_ref, grad_ref,
                 cnt_ref, tok_ref, cot_ref, win_ref, wout_ref, xs, t_ref, y_ref, z_ref, wz, w, work,
                 in_sem, tx_send, tx_recv, own_sem, z_send, z_recv, s_send, s_recv,
                 ry_send, ry_recv):
    c, f = lax.axis_index("clip"), lax.axis_index("frame")
    chip, core = f // 2, f % 2
    quad = c // 4
    twin = f + 1 - 2 * core
    loads = [pltpu.make_async_copy(src, dst, in_sem.at[k]) for k, (src, dst) in enumerate(
        ((win_hbm, win_ref), (wout_hbm, wout_ref), (tok_hbm.at[0, 0], tok_ref), (cot_hbm.at[0, 0], cot_ref), (cnt_hbm, cnt_ref)))]
    for load in loads:
        load.start()
    barrier = pltpu.get_barrier_semaphore()

    def hail(i, _):
        pl.semaphore_signal(barrier, inc=1, device_id=(c, (f + i) % 32), device_id_type=MESH)
        return 0
    zs = [(c + 4) % 16, (c + 12) % 16, (c + 8) % 16] + [4 * quad + (c + d) % 4 for d in (1, 2, 3)]
    for z in zs:
        pl.semaphore_signal(barrier, inc=1, device_id=(z, f), device_id_type=MESH)
    lax.fori_loop(1, 32, hail, 0)
    for load in loads:
        load.wait()
    wz[c, :, 0:192] = win_ref[...]
    wz[c, :, 192:256] = wout_ref[...]
    for src, at in ((tok_ref, 0), (cot_ref, 1)):
        xs[0:24, at] = src[0:192].reshape(24, 8, D)
        xs[24, at, 0:4] = src[192:196]
        xs[24, at, 4:8] = jnp.zeros((4, D), BF16)
    pl.semaphore_wait(barrier, 37)

    def remote(src, dst, send_sem, recv_sem, to):
        return pltpu.make_async_remote_copy(
            src_ref=src, dst_ref=dst, send_sem=send_sem, recv_sem=recv_sem, device_id=to, device_id_type=MESH)

    def far(k):
        ref = wz.at[c]
        return remote(ref, ref, z_send.at[k], z_recv.at[k], (zs[k], f))

    def near(wave, k):
        ref = wz.at[4 * ((quad + WAVES[wave]) % 4) + c % 4]
        n = 3 + 3 * wave + k
        return remote(ref, ref, z_send.at[n], z_recv.at[n], (zs[3 + k], f))

    for k in (2, 0, 1):
        far(k).start()
    for k in range(3):
        near(0, k).start()

    def tx(i):
        peer = (f + i) % 32
        j = worker_of(peer)
        return j, remote(xs.at[jnp.minimum(j, WORKERS - 1)], t_ref.at[f], tx_send.at[i], tx_recv.at[i], (c, peer))

    mine = worker_of(f)

    def tx_start(i, _):
        j, copy = tx(i)

        @pl.when(j < WORKERS)
        def _():
            copy.start()
        return 0

    own = pltpu.make_async_copy(xs.at[jnp.minimum(mine, WORKERS - 1)], t_ref.at[f], own_sem)

    lax.fori_loop(1, 32, tx_start, 0)
    own.start()

    def in_order(wave):
        low = lax.broadcasted_iota(jnp.int32, (32, 128), 1) < 64
        for k in range(2):
            z = 4 * ((quad + WAVES[wave]) % 4) + 2 * k
            first, second = wz[z].astype(F32), wz[z + 1].astype(F32)
            a0, a1, b0, b1 = first[:, :128], first[:, 128:], second[:, :128], second[:, 128:]
            turned = pltpu.roll(b0, 64, 1)
            parts = (a0, jnp.where(low, a1, turned), jnp.where(low, turned, pltpu.roll(b1, 64, 1)),
                     jnp.where(low, pltpu.roll(a1, 64, 1), b1))
            for j in range(4):
                for h in range(2):
                    w[chip, core, z + h, :, 128 * j:128 * j + 128] = parts[j][16 * h:16 * h + 16].astype(BF16)

    s1, s2 = 4 - 3 * core, 1 + 3 * core
    x, y = chip // 4, chip % 4
    a = x * (1 - core) + y * core
    b = y * (1 - core) + x * core

    def spot(da, db):
        return ((a + da) % 4) * s1 + ((b + db) % 4) * s2

    def theirs(da, db):
        return ((b + da) % 4) * s2 + ((a + db) % 4) * s1

    sent = []
    count = [0] * 4

    def block(wave, at, half, of_core):
        first = 4 * ((quad + WAVES[wave]) % 4)
        return w.at[at, of_core, pl.ds(first, 4) if half is None else pl.ds(first + 2 * half, 2)]

    def send(wave, at, to, sem, half=None):
        ref = block(wave, at, half, core)
        copy = remote(ref, ref, s_send.at[36 * wave + count[wave]], s_recv.at[36 * wave + sem], (c, to))
        copy.start()
        sent.append(copy)
        count[wave] += 1

    def take(wave, at, sem, half=None, of_core=core):
        ref = block(wave, at, half, of_core)
        remote(ref, ref, s_send.at[36 * wave], s_recv.at[36 * wave + sem], (c, twin)).wait_recv()

    an, ap, bn, bp = spot(-1, 0), spot(1, 0), spot(0, -1), spot(0, 1)
    to_an, to_ap, to_bn, to_bp = (2 * v + core for v in (an, ap, bn, bp))
    row = (0, -1, 1, 2)

    def along_b(v, n):
        send(v, spot(row[n], 0), to_bp, 4 + 4 * n)
        send(v, spot(row[n], 0), to_bn, 4 + 4 * n + 1)

    def own_out(v):
        for k in range(3):
            near(v, k).wait_recv()
        in_order(v)
        send(v, chip, to_ap, 0)
        send(v, chip, to_an, 1)
        along_b(v, 0)
        send(v, chip, twin, 20)

    def along_a(v):
        take(v, an, 0)
        send(v, an, to_ap, 2, 0)
        along_b(v, 1)
        send(v, an, twin, 21)
        take(v, ap, 1)
        send(v, ap, to_an, 3, 1)
        along_b(v, 2)
        send(v, ap, twin, 22)

    def across_a(v):
        take(v, spot(2, 0), 2, 0)
        take(v, spot(2, 0), 3, 1)
        along_b(v, 3)
        send(v, spot(2, 0), twin, 23)

    def from_b(v, n):
        take(v, spot(row[n], -1), 4 + 4 * n)
        send(v, spot(row[n], -1), to_bp, 4 + 4 * n + 2, 0)
        send(v, spot(row[n], -1), twin, 24 + 3 * n)
        take(v, spot(row[n], 1), 4 + 4 * n + 1)
        send(v, spot(row[n], 1), to_bn, 4 + 4 * n + 3, 1)
        send(v, spot(row[n], 1), twin, 25 + 3 * n)

    def across_b(v, n):
        take(v, spot(row[n], 2), 4 + 4 * n + 2, 0)
        take(v, spot(row[n], 2), 4 + 4 * n + 3, 1)
        send(v, spot(row[n], 2), twin, 26 + 3 * n)

    def pass_on(v, k):
        far(k).wait_recv()
        for i in range(3):
            near(v, i).start()

    cnt = cnt_ref[0]
    nrm, xhat, rstd, g, bias, proj, ga, att, dproj, gn = work

    def tokens_in():
        @pl.when(mine < WORKERS)
        def _():
            def tx_wait(i, _):
                remote(xs.at[0], t_ref.at[(f - i + 32) % 32], tx_send.at[i], tx_recv.at[i], (c, twin)).wait_recv()
                return 0
            lax.fori_loop(1, 32, tx_wait, 0)
        own.wait()

        @pl.when(mine < WORKERS)
        def _():
            norm_stage(t_ref, nrm, xhat, rstd, gain_ref)
            mask_stage(cnt, t_ref, g, bias)

    def finish(v):
        for n in range(4):
            take(v, theirs(row[n], 0), 20 + n, of_core=1 - core)
        for n in range(4):
            for k, db in enumerate((-1, 1, 2)):
                take(v, theirs(row[n], db), 24 + 3 * n + k, of_core=1 - core)

        @pl.when(mine < WORKERS)
        def _():
            project_stage((quad + WAVES[v]) % 4, nrm, w, proj)
            grad_attended_stage((quad + WAVES[v]) % 4, v == 0, g, w, gn)

    pass_on(1, 0)
    pass_on(2, 1)
    own_out(0)
    pass_on(3, 2)
    along_a(0)
    own_out(1)
    own_out(2)
    from_b(0, 0)
    across_a(0)
    own_out(3)
    along_a(1)
    along_a(2)
    from_b(0, 1)
    from_b(0, 2)
    along_a(3)
    from_b(1, 0)
    from_b(2, 0)
    across_a(1)
    across_a(2)
    from_b(0, 3)
    from_b(3, 0)
    across_a(3)
    across_b(0, 0)
    from_b(1, 1)
    from_b(2, 1)
    from_b(1, 2)
    from_b(2, 2)
    across_b(0, 1)
    across_b(0, 2)
    from_b(3, 1)
    from_b(3, 2)
    from_b(1, 3)
    from_b(2, 3)
    from_b(3, 3)
    across_b(0, 3)
    across_b(1, 0)
    across_b(1, 1)
    across_b(1, 2)
    across_b(1, 3)
    tokens_in()
    across_b(2, 0)
    across_b(2, 1)
    across_b(2, 2)
    across_b(2, 3)
    finish(0)
    across_b(3, 0)
    across_b(3, 1)
    across_b(3, 2)
    across_b(3, 3)
    finish(1)
    finish(2)
    finish(3)

    slot = jnp.minimum(mine, WORKERS - 1)

    def back(i, part):
        peer = (f + i) % 32
        return remote(y_ref.at[peer, part], z_ref.at[part, slot], ry_send.at[part, i], ry_recv.at[part, i], (c, peer))

    def keep(part):
        return pltpu.make_async_copy(y_ref.at[f, part], z_ref.at[part, slot], ry_send.at[part, 0])

    def give_result():
        def start(i, _):
            back(i, 0).start()
            return 0
        keep(0).start()
        lax.fori_loop(1, 32, start, 0)

    def give_grad(frame):
        @pl.when(frame == f)
        def _():
            keep(1).start()

        @pl.when(frame != f)
        def _():
            back((frame + 32 - f) % 32, 1).start()

    @pl.when(mine < WORKERS)
    def _():
        ga[...] = gn[...].astype(BF16)
        attention_stage(proj, ga, att, dproj, bias)
        result_stage(cnt, t_ref, att, w, y_ref)
        give_result()
        grad_stage(t_ref, dproj, w, xhat, rstd, gain_ref, gn, y_ref, f // 4, give_grad)

    for part, ref in ((0, res_ref), (1, grad_ref)):
        def wait(i, _):
            j = worker_of((f - i + 32) % 32)

            @pl.when(j < WORKERS)
            def _():
                remote(y_ref.at[0, part], z_ref.at[part, jnp.minimum(j, WORKERS - 1)],
                       ry_send.at[part, i], ry_recv.at[part, i], (c, twin)).wait_recv()
            return 0
        lax.fori_loop(1, 32, wait, 0)

        @pl.when(mine < WORKERS)
        def _():
            keep(part).wait()
        ref[0, 0, 0:192] = z_ref[part, 0:24].reshape(192, D)
        ref[0, 0, 192:196] = z_ref[part, 24, 0:4]

    @pl.when(mine < WORKERS)
    def _():
        def back_done(i, _):
            back(i, 0).wait_send()
            back(i, 1).wait_send()
            return 0
        lax.fori_loop(1, 32, back_done, 0)

    def tx_done(i, _):
        j, copy = tx(i)

        @pl.when(j < WORKERS)
        def _():
            copy.wait_send()
        return 0
    lax.fori_loop(1, 32, tx_done, 0)

    for k in range(3):
        far(k).wait_send()
        for v in range(4):
            near(v, k).wait_send()
    for copy in sent:
        copy.wait_send()


def per_device(tokens, counts, norm_gain, input_weights, output_weights, cotangent):
    dma = pltpu.SemaphoreType.DMA
    vm = pl.BlockSpec(memory_space=pltpu.VMEM)
    hbm = pl.BlockSpec(memory_space=pl.ANY)
    return tuple(pl.pallas_call(
        block_kernel,
        out_shape=(jax.ShapeDtypeStruct((1, 1, 196, D), BF16),) * 2,
        in_specs=[hbm, vm, hbm, hbm, hbm, hbm], out_specs=(vm, vm),
        scratch_shapes=[
            pltpu.SMEM((1,), jnp.int32), pltpu.VMEM((196, D), BF16), pltpu.VMEM((196, D), BF16), pltpu.VMEM((32, 192), BF16), pltpu.VMEM((32, 64), BF16),
            pltpu.VMEM((WORKERS, 2, 8, D), BF16), pltpu.VMEM((32, 2, 8, D), BF16), pltpu.VMEM((32, 2, 8, D), BF16),
            pltpu.VMEM((2, WORKERS, 8, D), BF16), pltpu.VMEM((16, 32, 256), BF16),
            pltpu.VMEM((16, 2, 16, 16, 512), BF16), SCRATCH,
            dma((5,)), dma((32,)), dma((32,)), dma, dma((15,)), dma((15,)), dma((144,)), dma((144,)),
            dma((2, 32)), dma((2, 32))],
        compiler_params=pltpu.CompilerParams(collective_id=0, has_side_effects=True, vmem_limit_bytes=VMEM_MB << 20),
        name="temporal_block",
    )(counts, norm_gain.reshape(1, D), tokens, cotangent, input_weights, output_weights))


def solution(mesh):
    rows = P("clip", "frame", None, None)
    return jax.shard_map(
        per_device, mesh=mesh,
        in_specs=(rows, P("clip"), P(), P("frame", "clip"), P("frame", "clip"), rows),
        out_specs=(rows, rows), check_vma=False)
```
